256 devices in a mesh: row: 32 (over y_lo, z, core), col: 8 (over x, y_hi).
Axes of the slice: x: 4, y: 4 (y_hi: 2, y_lo: 2; y = y_hi * 2 + y_lo), z: 8, core: 2. Of those that a mesh axis runs over, the one named last changes fastest.
Arguments:
- start_block: float32 [32768, 256], P(('row', 'col')), may hold values from -6 to 6
- tiles: bfloat16 [32, 8, 14, 128, 128], P('row', 'col'), may hold values from -0.125 to 0.125
- tile_rows: int32 [32, 8, 14], P('row', 'col'), may hold values from -1 to 255, as said below
- tile_cols: int32 [32, 8, 14], P('row', 'col'), may hold values from -1 to 255, as said below
- bounds: float32 [3], replicated, may hold values from -2.6 to 2.6, as said below
Outputs:
- filtered: float32 [32768, 256], P(('row', 'col'))
The draws below stay inside these ranges and needn't reach their ends.
Inputs may be any that keep to these rules, and one draw needn't show every extreme that they name: Vector rows form blocks of 128 rows, one block a device, in row+col order. On the device at grid row r and grid column c, a live slot names a block row held by one of the devices (r, any column) and a block column held by one of the devices (any row, c). Live slots come first; each device has 1 to 14 live slots, and one device has exactly 14 in every draw. No block position is named twice, and the mirror of a named position is never named unless it lies on the diagonal. tile_rows and tile_cols are -1 together. `tile_cols`: same slots as tile_rows. bounds[0] < bounds[1] < bounds[2].
All inputs are finite; a program needn't handle non-finite values.
Results may differ from the reference program's by a relative error of at most 0.0042.
Values may be sent and summed in bfloat16 or wider, within the bound.
No kernel may reach another device: no remote copies, remote signals or barrier semaphores. Data moves between devices by JAX's collectives and lax.ppermute only.
A program may use at most 64 MiB of HBM per device.

```python
import jax
import jax.numpy as jnp
from jax import lax

K = 256
TILE = 128
BLK_DEV = 1
TILES_DEV = 14
DEGREE = 4
ORDER = 32768
N_ROW = 32
N_COL = 8


def tile_pattern(key):
    base = jax.random.fold_in(key, 7)
    group_count = N_ROW * N_COL
    near_count = N_COL * BLK_DEV
    far_count = N_ROW * BLK_DEV
    positions = near_count * far_count
    shape = (N_ROW, N_COL, near_count, far_count)
    row_grid = lax.broadcasted_iota(jnp.int32, shape, 0)
    col_grid = lax.broadcasted_iota(jnp.int32, shape, 1)
    near_grid = lax.broadcasted_iota(jnp.int32, shape, 2)
    far_grid = lax.broadcasted_iota(jnp.int32, shape, 3)
    glob_i = row_grid * near_count + near_grid
    glob_j = (far_grid // BLK_DEV * N_COL + col_grid) * BLK_DEV + far_grid % BLK_DEV
    parity = (glob_i + glob_j) % 2
    keep = (glob_i == glob_j) | (glob_i < glob_j) & (parity == 0) | (glob_i > glob_j) & (parity == 1)
    upper = max(2, (1 << 30) // positions)
    flat_index = near_grid * far_count + far_grid
    scores = jax.random.randint(jax.random.fold_in(base, 1), shape, 0, upper) * positions + flat_index
    scores = jnp.where(keep, scores, -1).reshape(N_ROW, N_COL, positions)
    chosen_scores, chosen = lax.top_k(scores, TILES_DEV)
    chosen = chosen.astype(jnp.int32)
    counts = jax.random.randint(jax.random.fold_in(base, 2), (N_ROW, N_COL), TILES_DEV // 8, TILES_DEV + 1)
    full_device = jax.random.randint(jax.random.fold_in(base, 3), (), 0, group_count)
    device_ids = lax.broadcasted_iota(jnp.int32, (N_ROW, N_COL), 0) * N_COL + lax.broadcasted_iota(jnp.int32, (N_ROW, N_COL), 1)
    counts = jnp.where(device_ids == full_device, TILES_DEV, counts)
    slot_shape = (N_ROW, N_COL, TILES_DEV)
    slot_ids = lax.broadcasted_iota(jnp.int32, slot_shape, 2)
    alive = slot_ids < counts[:, :, None]
    near_sel = chosen // far_count
    far_sel = chosen % far_count
    row_slot = lax.broadcasted_iota(jnp.int32, slot_shape, 0)
    col_slot = lax.broadcasted_iota(jnp.int32, slot_shape, 1)
    glob_rows = row_slot * near_count + near_sel
    glob_cols = (far_sel // BLK_DEV * N_COL + col_slot) * BLK_DEV + far_sel % BLK_DEV
    return (jnp.where(alive, glob_rows, -1), jnp.where(alive, glob_cols, -1))


def draw_tile_rows(key, part):
    return tile_pattern(key)[0]


def draw_tile_cols(key, part):
    return tile_pattern(key)[1]


def draw_bounds(key, part):
    uniform_part = jax.random.uniform(jax.random.fold_in(key, 11), (3,), jnp.float32)
    lowest = jnp.array([-2.6, -1.2, 2.3], jnp.float32)
    spread = jnp.array([0.3, 0.4, 0.3], jnp.float32)
    return lowest + uniform_part * spread


def block_levels(key, dims, shards, smallest, high):
    def one(dim, shards_of):
        heights = jax.random.uniform(jax.random.fold_in(jax.random.fold_in(key, 6), dim), (shards_of,), jnp.float32, smallest / len(shards), high / len(shards))
        return jnp.repeat(jnp.exp(heights), dims[dim] // shards_of).reshape((-1,) + (1,) * (len(dims) - dim - 1))

    factor_of = one(*shards[0])
    for cut in shards[1:]:
        factor_of = factor_of * one(*cut)
    return factor_of


def gaussian(own_key, shape, scale, limit, pieces=(), kind=jnp.bfloat16):
    result = jax.random.normal(own_key, shape, jnp.float32) * scale
    if len(pieces) > 0:
        result = block_levels(own_key, shape, pieces, -0.22, 0.18) * result
    return jnp.clip(result, min=-limit, max=limit).astype(kind)


def setup_inputs(seed: int = 0) -> dict:
    key_list = jax.random.split(jax.random.key(seed), 6)
    return {
        "start_block": gaussian(key_list[0], (ORDER, K), 1.0, 6.0, ((0, 256),), jnp.float32),
        "tiles": gaussian(key_list[1], (N_ROW, N_COL, TILES_DEV, TILE, TILE), (TILE * 9 * TILES_DEV // (8 * BLK_DEV)) ** -0.5, 0.125, ((0, 32), (1, 8))),
        "tile_rows": draw_tile_rows(jax.random.fold_in(key_list[5], 71), 0),
        "tile_cols": draw_tile_cols(jax.random.fold_in(key_list[5], 71), 0),
        "bounds": draw_bounds(jax.random.fold_in(key_list[5], 71), 0),
    }


def apply_matrix(vectors, tiles, tile_rows, tile_cols):
    block_count = N_ROW * N_COL * BLK_DEV
    group_count = N_ROW * N_COL
    low_vectors = lax.optimization_barrier(vectors.astype(jnp.bfloat16))
    blocks_f = low_vectors.astype(jnp.float32).reshape(block_count, TILE, K)
    tile_sets = tiles.reshape(group_count, TILES_DEV, TILE, TILE)
    row_sets = tile_rows.reshape(group_count, TILES_DEV)
    col_sets = tile_cols.reshape(group_count, TILES_DEV)

    def one_group(accum, item):
        tile_mats, rows_here, cols_here = item
        tile_f = tile_mats.astype(jnp.float32)
        is_live = rows_here >= 0
        rows_safe = jnp.maximum(rows_here, 0)
        cols_safe = jnp.maximum(cols_here, 0)
        forward = jnp.einsum('txy,tyk->txk', tile_f, blocks_f[cols_safe], precision=lax.Precision.HIGHEST)
        backward = jnp.einsum('tyx,tyk->txk', tile_f, blocks_f[rows_safe], precision=lax.Precision.HIGHEST)
        accum = accum.at[jnp.where(is_live, rows_here, block_count)].add(forward, mode="drop")
        accum = accum.at[jnp.where(is_live, cols_here, block_count)].add(backward, mode="drop")
        return accum, None

    start = jnp.zeros((block_count, TILE, K), jnp.float32)
    accum, _ = lax.scan(one_group, start, (tile_sets, row_sets, col_sets))
    return accum.reshape(block_count * TILE, K)


def reference(start_block, tiles, tile_rows, tile_cols, bounds):
    half_width = (bounds[2] - bounds[1]) * 0.5
    center = (bounds[2] + bounds[1]) * 0.5
    sigma_one = half_width / (bounds[0] - center)
    previous = start_block
    current = (apply_matrix(start_block, tiles, tile_rows, tile_cols) - center * start_block) * (sigma_one / half_width)
    sigma = sigma_one
    for turn_index in range(DEGREE - 1):
        sigma_next = 1.0 / (2.0 / sigma_one - sigma)
        product = apply_matrix(current, tiles, tile_rows, tile_cols)
        following = (product - center * current) * (2.0 * sigma_next / half_width) - (sigma * sigma_next) * previous
        previous = current
        current = following
        sigma = sigma_next
    return current
```

```python
import functools

import jax
import jax.numpy as jnp
from jax import lax
from jax.experimental import pallas as pl
from jax.experimental.pallas import tpu as pltpu
from jax.sharding import Mesh
from jax.sharding import PartitionSpec as P

DEGREE = 4
BATCH = 8
SIZES = {"yl": 2, "zh": 4, "zl": 2, "core": 2, "x": 4, "yh": 2}
GROUP = ("yl", "yh", "zl")
CHIPS = 8
BLOCKS = 2 * CHIPS
RING = 4
SUMS = RING * BLOCKS
LIST = 256


def shift_y(array, step):
    pairs = []
    for low in range(2):
        for high in range(2):
            target = (high * 2 + low - step) % 4
            pairs.append((low * 2 + high, target % 2 * 2 + target // 2))
    return lax.ppermute(array, ("yl", "yh"), pairs)


def swap(array, axis):
    return lax.ppermute(array, axis, [(0, 1), (1, 0)])


def exchange(array, step, x_core):
    pairs = []
    for high in range(RING):
        for core in range(2):
            for place in range(RING):
                if core == x_core:
                    target = (high * 2 + core) * RING + (place + step) % RING
                else:
                    target = ((high + step) % RING * 2 + core) * RING + place
                pairs.append(((high * 2 + core) * RING + place, target))
    return lax.ppermute(array, ("zh", "core", "x"), pairs)


def list_kernel(slots, meta, where, jobs, count):
    core, high, place, along_y, low = (where[i] for i in range(5))

    def source(piece, found):
        core_s = core ^ (piece >> 3)
        low_s = low ^ ((piece >> 2) & 1)
        y_s = (along_y + (piece & 3)) & 3
        block_s = core_s * 8 + ((y_s & 1) * 2 + (y_s >> 1)) * 2 + low_s

        def slot(t, found):
            row = meta[block_s * 2 * slots + t]
            col = meta[(block_s * 2 + 1) * slots + t]
            spots = []
            for number in (row, col):
                group, member = number >> 3, number & 7
                block = (
                    (group & 1) * 8
                    + ((group >> 4) * 2 + (member & 1)) * 2
                    + ((group >> 1) & 1)
                )
                spots.append((block, (group >> 2) & 3, member >> 1))
            near = ((spots[0][2] - place) & 3) * BLOCKS + spots[0][0]
            far = ((spots[1][1] - high) & 3) * BLOCKS + spots[1][0]
            taken = jnp.where(core == 0, near, far)
            given = jnp.where(core == 0, far, near)
            jobs[found] = ((piece * slots + t) << 16) | (taken << 8) | given
            return found + jnp.where(row >= 0, 1, 0)

        return lax.fori_loop(0, slots, slot, found)

    found = lax.fori_loop(0, BLOCKS, source, jnp.int32(0))
    for extra in range(BATCH):
        jobs[found + extra] = SUMS
    count[0] = (found + BATCH - 1) // BATCH


def apply_kernel(jobs, count, where, tiles, *refs):
    taken = refs[:RING]
    given = refs[RING : 2 * RING]
    vectors, sums = refs[2 * RING :]
    for d in range(RING):
        vectors[d * BLOCKS : (d + 1) * BLOCKS] = taken[d][...]
    sums[...] = jnp.zeros_like(sums)

    def multiply(contract):
        def batch(step, carry):
            products = []
            for k in range(BATCH):
                job = jobs[step * BATCH + k]
                products.append(
                    (
                        job & 255,
                        lax.dot_general(
                            vectors[(job >> 8) & 255],
                            tiles[job >> 16],
                            (((1,), (contract,)), ((), ())),
                            preferred_element_type=jnp.float32,
                        ),
                    )
                )
            for spot, product in products:
                sums[spot] += product
            return carry

        lax.fori_loop(0, count[0], batch, 0)

    @pl.when(where[0] == 0)
    def _():
        multiply(0)

    @pl.when(where[0] != 0)
    def _():
        multiply(1)

    for d in range(RING):
        given[d][...] = sums[d * BLOCKS : (d + 1) * BLOCKS].astype(given[d].dtype)


def local(start_block, tiles, tile_rows, tile_cols, bounds):
    size, width = start_block.shape
    slots = tiles.shape[2]
    part = width // CHIPS
    spot = {name: lax.axis_index(name) for name in SIZES}
    core = spot["core"]
    where = jnp.stack(
        [core, spot["zh"], spot["x"], spot["yh"] * 2 + spot["yl"], spot["zl"]]
    ).astype(jnp.int32)

    own_tiles = tiles.reshape(slots, size, size)
    places = jnp.concatenate(
        [tile_rows.reshape(1, slots), tile_cols.reshape(1, slots)]
    ).astype(jnp.float32)
    places = jnp.pad(places, ((0, 6), (0, size - slots)))
    message = jnp.concatenate(
        [
            start_block.T.reshape(CHIPS, part, size),
            jnp.broadcast_to(places[None], (CHIPS, 8, size)),
        ],
        axis=1,
    )
    mine = lax.all_to_all(message, GROUP, 0, 0)
    theirs = swap(mine, "core")
    first = jnp.where(core == 0, mine, theirs)
    second = jnp.where(core == 0, theirs, mine)
    dealt = jnp.concatenate([first, second])
    start = dealt[:, :part]
    meta = dealt[:, part : part + 2, :slots].astype(jnp.int32).reshape(-1)

    half = slots // 2
    beside = swap(own_tiles, "zl")
    up, down = shift_y(own_tiles, 1), shift_y(own_tiles, -1)
    beside_up, beside_down = shift_y(beside, 1), shift_y(beside, -1)
    over = shift_y(up[:half], 1), shift_y(down[half:], -1)
    beside_over = swap(over[0], "zl"), swap(over[1], "zl")
    pieces = [own_tiles, up, *over, down, beside, beside_up, *beside_over, beside_down]
    all_tiles = jnp.concatenate(pieces + [swap(piece, "core") for piece in pieces])

    smem = pl.BlockSpec(memory_space=pltpu.SMEM)
    vmem = pl.BlockSpec(memory_space=pltpu.VMEM)
    jobs, count = pl.pallas_call(
        functools.partial(list_kernel, slots),
        out_shape=(
            jax.ShapeDtypeStruct((LIST,), jnp.int32),
            jax.ShapeDtypeStruct((1,), jnp.int32),
        ),
        in_specs=[smem, smem],
        out_specs=(smem, smem),
        name="list_jobs",
    )(meta, where)
    apply_tiles = pl.pallas_call(
        apply_kernel,
        out_shape=[jax.ShapeDtypeStruct((BLOCKS, part, size), jnp.float32)]
        + [jax.ShapeDtypeStruct((BLOCKS, part, size), jnp.bfloat16)] * (RING - 1),
        in_specs=[smem, smem, smem] + [vmem] * (1 + RING),
        out_specs=[vmem] * RING,
        scratch_shapes=[
            pltpu.VMEM((SUMS, part, size), jnp.bfloat16),
            pltpu.VMEM((SUMS + 1, part, size), jnp.float32),
        ],
        compiler_params=pltpu.CompilerParams(vmem_limit_bytes=32 << 20),
        name="apply_tiles",
    )

    def apply_matrix(vectors):
        low = vectors.astype(jnp.bfloat16)
        gathered = {d: exchange(low, -d, 0) for d in (2, 1, 3)}
        total, *partial = apply_tiles(
            jobs, count, where, all_tiles, low, *(gathered[d] for d in (1, 2, 3))
        )
        sent = [exchange(partial[d - 1], d, 1) for d in (2, 1, 3)]
        for piece in sent:
            total = total + piece.astype(jnp.float32)
        return total + swap(total, "core")

    half_width = (bounds[2] - bounds[1]) * 0.5
    center = (bounds[2] + bounds[1]) * 0.5
    sigma_one = half_width / (bounds[0] - center)
    previous = start
    current = (apply_matrix(start) - center * start) * (sigma_one / half_width)
    sigma = sigma_one
    for _ in range(DEGREE - 1):
        sigma_next = 1.0 / (2.0 / sigma_one - sigma)
        product = apply_matrix(current)
        following = (product - center * current) * (2.0 * sigma_next / half_width) - (
            sigma * sigma_next
        ) * previous
        previous = current
        current = following
        sigma = sigma_next
    keep = jnp.where(core == 0, current[:CHIPS], current[CHIPS:])
    back = lax.all_to_all(keep, GROUP, 0, 0)
    return back.reshape(width, size).T


def solution(mesh):
    fine = Mesh(mesh.devices.reshape(tuple(SIZES.values())), tuple(SIZES))
    row, col = ("yl", "zh", "zl", "core"), ("x", "yh")
    placed = (
        P(row + col, None),
        P(row, col, None, None, None),
        P(row, col, None),
        P(row, col, None),
        P(),
    )
    return jax.shard_map(
        local, mesh=fine, in_specs=placed, out_specs=P(row + col, None), check_vma=False
    )
```

```python
import functools

import jax
import jax.numpy as jnp
from jax import lax
from jax.experimental import pallas as pl
from jax.experimental.pallas import tpu as pltpu
from jax.sharding import Mesh
from jax.sharding import PartitionSpec as P

DEGREE = 4
BATCH = 8
SIZES = {"yl": 2, "zh": 4, "zl": 2, "core": 2, "x": 4, "yh": 2}
GROUP = ("yl", "yh", "zl")
CHIPS = 8
BLOCKS = 2 * CHIPS
RING = 4
SUMS = RING * BLOCKS
LIST = 256
STAGE = 2


def swap(array, axis):
    return lax.ppermute(array, axis, [(0, 1), (1, 0)])


def exchange(array, step, x_core):
    pairs = []
    for high in range(RING):
        for core in range(2):
            for place in range(RING):
                if core == x_core:
                    target = (high * 2 + core) * RING + (place + step) % RING
                else:
                    target = ((high + step) % RING * 2 + core) * RING + place
                pairs.append(((high * 2 + core) * RING + place, target))
    return lax.ppermute(array, ("zh", "core", "x"), pairs)


def list_kernel(slots, meta, where, jobs, marks):
    core, high, place = (where[i] for i in range(3))

    def source(piece, found):
        def slot(t, found):
            row = meta[piece * 2 * slots + t]
            col = meta[(piece * 2 + 1) * slots + t]
            spots = []
            for number in (row, col):
                group, member = number >> 3, number & 7
                block = (
                    (group & 1) * 8
                    + ((group >> 4) * 2 + (member & 1)) * 2
                    + ((group >> 1) & 1)
                )
                spots.append((block, (group >> 2) & 3, member >> 1))
            near = ((spots[0][2] - place) & 3) * BLOCKS + spots[0][0]
            far = ((spots[1][1] - high) & 3) * BLOCKS + spots[1][0]
            taken = jnp.where(core == 0, near, far)
            given = jnp.where(core == 0, far, near)
            jobs[found] = ((piece * slots + t) << 16) | (taken << 8) | given
            return found + jnp.where(row >= 0, 1, 0)

        found = lax.fori_loop(0, slots, slot, found)
        marks[piece] = found // BATCH
        return found

    found = lax.fori_loop(0, BLOCKS, source, jnp.int32(0))
    for extra in range(BATCH):
        jobs[found + extra] = SUMS
    marks[BLOCKS - 1] = (found + BATCH - 1) // BATCH


def apply_kernel(jobs, marks, where, gathered, *refs):
    taken, given = refs[:RING], refs[RING : 2 * RING]
    vectors, sums, tiles, arrived = refs[2 * RING :]
    chunk = tiles.shape[0] // BLOCKS * STAGE
    copies = []
    for k in range(BLOCKS // STAGE):
        part = pl.ds(k * chunk, chunk)
        copies.append(
            pltpu.make_async_copy(gathered.at[part], tiles.at[part], arrived.at[k])
        )
        copies[-1].start()
    for d in range(RING):
        vectors[d * BLOCKS : (d + 1) * BLOCKS] = taken[d][...]
    sums[...] = jnp.zeros_like(sums)

    def batches(first, last, contract):
        def batch(step, carry):
            products = []
            for k in range(BATCH):
                job = jobs[step * BATCH + k]
                products.append(
                    (
                        job & 255,
                        lax.dot_general(
                            vectors[(job >> 8) & 255],
                            tiles[job >> 16],
                            (((1,), (contract,)), ((), ())),
                            preferred_element_type=jnp.float32,
                        ),
                    )
                )
            for spot, product in products:
                sums[spot] += product
            return carry

        lax.fori_loop(first, last, batch, 0)

    first = 0
    for stage, copy in enumerate(copies):
        copy.wait()
        last = marks[stage * STAGE + STAGE - 1]

        @pl.when(where[0] == 0)
        def _():
            batches(first, last, 0)

        @pl.when(where[0] != 0)
        def _():
            batches(first, last, 1)

        first = last

    for d in range(RING):
        given[d][...] = sums[d * BLOCKS : (d + 1) * BLOCKS].astype(given[d].dtype)


def local(start_block, tiles, tile_rows, tile_cols, bounds):
    size, width = start_block.shape
    slots = tiles.shape[2]
    part = width // CHIPS
    spot = {name: lax.axis_index(name) for name in SIZES}
    core = spot["core"]
    where = jnp.stack([core, spot["zh"], spot["x"]]).astype(jnp.int32)

    own_tiles = tiles.reshape(slots, size, size)
    places = jnp.concatenate(
        [tile_rows.reshape(1, slots), tile_cols.reshape(1, slots)]
    ).astype(jnp.float32)
    places = jnp.pad(places, ((0, 6), (0, size - slots)))
    message = jnp.concatenate(
        [
            start_block.T.reshape(CHIPS, part, size),
            jnp.broadcast_to(places[None], (CHIPS, 8, size)),
        ],
        axis=1,
    )
    mine = lax.all_to_all(message, GROUP, 0, 0)
    theirs = swap(mine, "core")
    first = jnp.where(core == 0, mine, theirs)
    second = jnp.where(core == 0, theirs, mine)
    dealt = jnp.concatenate([first, second])
    start = dealt[:, :part]
    meta = dealt[:, part : part + 2, :slots].astype(jnp.int32).reshape(-1)

    all_tiles = lax.all_gather(own_tiles, ("core",) + GROUP, axis=0, tiled=True)
    stored_tiles = pltpu.with_memory_space_constraint(all_tiles, pltpu.HBM)

    smem = pl.BlockSpec(memory_space=pltpu.SMEM)
    vmem = pl.BlockSpec(memory_space=pltpu.VMEM)
    jobs, marks = pl.pallas_call(
        functools.partial(list_kernel, slots),
        out_shape=(
            jax.ShapeDtypeStruct((LIST,), jnp.int32),
            jax.ShapeDtypeStruct((BLOCKS,), jnp.int32),
        ),
        in_specs=[smem, smem],
        out_specs=(smem, smem),
        name="list_jobs",
    )(meta, where)
    apply_tiles = pl.pallas_call(
        apply_kernel,
        out_shape=[jax.ShapeDtypeStruct((BLOCKS, part, size), jnp.float32)]
        + [jax.ShapeDtypeStruct((BLOCKS, part, size), jnp.bfloat16)] * (RING - 1),
        in_specs=[smem] * 3
        + [pl.BlockSpec(memory_space=pltpu.HBM)]
        + [vmem] * RING,
        out_specs=[vmem] * RING,
        scratch_shapes=[
            pltpu.VMEM((SUMS, part, size), jnp.bfloat16),
            pltpu.VMEM((SUMS + 1, part, size), jnp.float32),
            pltpu.VMEM((BLOCKS * slots, size, size), jnp.bfloat16),
            pltpu.SemaphoreType.DMA((BLOCKS // STAGE,)),
        ],
        compiler_params=pltpu.CompilerParams(vmem_limit_bytes=32 << 20),
        name="apply_tiles",
    )

    def apply_matrix(vectors):
        low = vectors.astype(jnp.bfloat16)
        gathered = {d: exchange(low, -d, 0) for d in (2, 1, 3)}
        total, *partial = apply_tiles(
            jobs, marks, where, stored_tiles, low, *(gathered[d] for d in (1, 2, 3))
        )
        sent = [exchange(partial[d - 1], d, 1) for d in (2, 1, 3)]
        for piece in sent:
            total = total + piece.astype(jnp.float32)
        return total + swap(total, "core")

    half_width = (bounds[2] - bounds[1]) * 0.5
    center = (bounds[2] + bounds[1]) * 0.5
    sigma_one = half_width / (bounds[0] - center)
    previous = start
    current = (apply_matrix(start) - center * start) * (sigma_one / half_width)
    sigma = sigma_one
    for _ in range(DEGREE - 1):
        sigma_next = 1.0 / (2.0 / sigma_one - sigma)
        product = apply_matrix(current)
        following = (product - center * current) * (2.0 * sigma_next / half_width) - (
            sigma * sigma_next
        ) * previous
        previous = current
        current = following
        sigma = sigma_next
    keep = jnp.where(core == 0, current[:CHIPS], current[CHIPS:])
    back = lax.all_to_all(keep, GROUP, 0, 0)
    return back.reshape(width, size).T


def solution(mesh):
    fine = Mesh(mesh.devices.reshape(tuple(SIZES.values())), tuple(SIZES))
    row, col = ("yl", "zh", "zl", "core"), ("x", "yh")
    placed = (
        P(row + col, None),
        P(row, col, None, None, None),
        P(row, col, None),
        P(row, col, None),
        P(),
    )
    return jax.shard_map(
        local, mesh=fine, in_specs=placed, out_specs=P(row + col, None), check_vma=False
    )
```

```python
import functools

import jax
import jax.numpy as jnp
from jax import lax
from jax.experimental import pallas as pl
from jax.experimental.pallas import tpu as pltpu
from jax.sharding import Mesh
from jax.sharding import PartitionSpec as P

DEGREE = 4
BATCH = 8
SIZES = {"yl": 2, "zh": 4, "zl": 2, "core": 2, "x": 4, "yh": 2}
GROUP = ("yl", "yh", "zl")
CHIPS = 8
BLOCKS = 2 * CHIPS
RING = 4
SUMS = RING * BLOCKS
LIST = 256


def around_y(array):
    pairs = []
    for low in range(2):
        for core in range(2):
            for high in range(2):
                target = (high * 2 + low - 1 + 2 * core) % 4
                pairs.append(
                    (
                        (low * 2 + core) * 2 + high,
                        (target % 2 * 2 + core) * 2 + target // 2,
                    )
                )
    return lax.ppermute(array, ("yl", "core", "yh"), pairs)


def swap(array, axis):
    return lax.ppermute(array, axis, [(0, 1), (1, 0)])


def exchange(array, step, x_core):
    pairs = []
    for high in range(RING):
        for core in range(2):
            for place in range(RING):
                if core == x_core:
                    target = (high * 2 + core) * RING + (place + step) % RING
                else:
                    target = ((high + step) % RING * 2 + core) * RING + place
                pairs.append(((high * 2 + core) * RING + place, target))
    return lax.ppermute(array, ("zh", "core", "x"), pairs)


def gather_vectors(low):
    return {d: exchange(low, -d, 0) for d in (2, 1, 3)}


def list_kernel(slots, codes, jobs, marks):
    def source(unit, found):
        def slot(t, found):
            code = codes[unit * slots + t]
            jobs[found] = code
            return found + jnp.where(code >= 0, 1, 0)

        found = lax.fori_loop(0, slots, slot, found)
        marks[unit] = found // BATCH
        return found

    found = lax.fori_loop(0, BLOCKS, source, jnp.int32(0))
    for extra in range(BATCH):
        jobs[found + extra] = SUMS
    marks[BLOCKS - 1] = (found + BATCH - 1) // BATCH


def apply_kernel(slots, units, jobs, marks, where, *refs):
    pieces, refs = refs[: len(units)], refs[len(units) :]
    taken, given = refs[:RING], refs[RING : 2 * RING]
    vectors, sums, tiles, arrived = refs[2 * RING :]
    copies, ends = [], []
    for k, (piece, count) in enumerate(zip(pieces, units)):
        part = pl.ds((ends[-1] if ends else 0) * slots, count * slots)
        copies.append(pltpu.make_async_copy(piece, tiles.at[part], arrived.at[k]))
        copies[-1].start()
        ends.append((ends[-1] if ends else 0) + count)
    for d in range(RING):
        vectors[d * BLOCKS : (d + 1) * BLOCKS] = taken[d][...]
    sums[...] = jnp.zeros_like(sums)

    def batches(first, last, contract):
        def batch(step, carry):
            products = []
            for k in range(BATCH):
                job = jobs[step * BATCH + k]
                products.append(
                    (
                        job & 255,
                        lax.dot_general(
                            vectors[(job >> 8) & 255],
                            tiles[job >> 16],
                            (((1,), (contract,)), ((), ())),
                            preferred_element_type=jnp.float32,
                        ),
                    )
                )
            for spot, product in products:
                sums[spot] += product
            return carry

        lax.fori_loop(first, last, batch, 0)

    first = 0
    for copy, end in zip(copies, ends):
        copy.wait()
        last = marks[end - 1]

        @pl.when(where[0] == 0)
        def _():
            batches(first, last, 0)

        @pl.when(where[0] != 0)
        def _():
            batches(first, last, 1)

        first = last

    for d in range(RING):
        given[d][...] = sums[d * BLOCKS : (d + 1) * BLOCKS].astype(given[d].dtype)


def local(start_block, tiles, tile_rows, tile_cols, bounds):
    size, width = start_block.shape
    slots = tiles.shape[2]
    part = width // CHIPS
    spot = {name: lax.axis_index(name) for name in SIZES}
    core = spot["core"]
    where = core.reshape(1).astype(jnp.int32)

    own_tiles = tiles.reshape(slots, size, size)
    places = jnp.concatenate(
        [tile_rows.reshape(1, slots), tile_cols.reshape(1, slots)]
    ).astype(jnp.float32)
    places = jnp.pad(places, ((0, 6), (0, size - slots)))
    message = jnp.concatenate(
        [
            start_block.T.reshape(CHIPS, part, size),
            jnp.broadcast_to(places[None], (CHIPS, 8, size)),
        ],
        axis=1,
    )
    def in_order(mine, theirs):
        return jnp.concatenate(
            [jnp.where(core == 0, mine, theirs), jnp.where(core == 0, theirs, mine)]
        )

    fellow = swap(own_tiles, "core")
    message, pair = lax.optimization_barrier((message, in_order(own_tiles, fellow)))
    around = around_y(pair)
    mine = lax.all_to_all(message, GROUP, 0, 0)
    theirs = swap(mine, "core")
    first = jnp.where(core == 0, mine, theirs)
    second = jnp.where(core == 0, theirs, mine)
    dealt = jnp.concatenate([first, second])
    start = dealt[:, :part]
    meta = dealt[:, part : part + 2, :slots].astype(jnp.int32)

    beside = swap(own_tiles, "zl")
    beside_fellow = swap(beside, "core")
    onward, dealt = lax.optimization_barrier(
        (jnp.where(core == 0, around[:slots], around[slots:]), dealt)
    )
    over = around_y(onward)
    low_start = dealt[:, :part].astype(jnp.bfloat16)
    first_gathered = gather_vectors(low_start)
    over, beside_pair, first_gathered = lax.optimization_barrier(
        (over, in_order(beside, beside_fellow), first_gathered)
    )
    beside_around = around_y(beside_pair)
    beside_over = swap(over, "zl")
    units = [1, 1, 1, 1, 2, 2, 1, 1, 2, 2, 1, 1]
    on_y, on_low = spot["yh"] * 2 + spot["yl"], spot["zl"]

    def unit(along, low, core_of):
        y = (on_y + along) % 4
        return core_of * CHIPS + (y % 2 * 2 + y // 2) * 2 + (on_low + low) % 2

    ahead = 1 - 2 * core
    held = [unit(0, low, c) for low in range(2) for c in (core, 1 - core)]
    for low in range(2):
        held += [unit(step, low, c) for step in (ahead, -ahead) for c in range(2)]
        held += [unit(2, low, c) for c in (core, 1 - core)]
    held = jnp.stack(held)

    group, member = meta >> 3, meta & 7
    block = (group & 1) * CHIPS + (
        ((group >> 4) * 2 + (member & 1)) * 2 + ((group >> 1) & 1)
    )
    near = ((member[:, 0] >> 1) - spot["x"] & 3) * BLOCKS + block[:, 0]
    far = ((group[:, 1] >> 2) - spot["zh"] & 3) * BLOCKS + block[:, 1]
    spots = jnp.where(core == 0, near << 8 | far, far << 8 | near)
    spots = jnp.where(meta[:, 0] >= 0, spots, -1)
    matches = held[:, None] == jnp.arange(BLOCKS, dtype=jnp.int32)[None]
    spots = jnp.sum(jnp.where(matches[:, :, None], spots[None], 0), axis=1)
    lies = jnp.arange(BLOCKS * slots, dtype=jnp.int32)
    codes = jnp.where(spots.reshape(-1) >= 0, lies << 16 | spots.reshape(-1), -1)

    smem = pl.BlockSpec(memory_space=pltpu.SMEM)
    vmem = pl.BlockSpec(memory_space=pltpu.VMEM)
    jobs, marks = pl.pallas_call(
        functools.partial(list_kernel, slots),
        out_shape=(
            jax.ShapeDtypeStruct((LIST,), jnp.int32),
            jax.ShapeDtypeStruct((BLOCKS,), jnp.int32),
        ),
        in_specs=[smem],
        out_specs=(smem, smem),
        name="list_jobs",
    )(codes)
    beside_around, beside_over, jobs, marks = lax.optimization_barrier(
        (beside_around, beside_over, jobs, marks)
    )
    pieces = [own_tiles, fellow, beside, beside_fellow, around, swap(around, "core")]
    pieces += [over, swap(over, "core"), beside_around, swap(beside_around, "core")]
    pieces += [beside_over, swap(beside_over, "core")]
    stored = [pltpu.with_memory_space_constraint(p, pltpu.HBM) for p in pieces]
    apply_tiles = pl.pallas_call(
        functools.partial(apply_kernel, slots, units),
        out_shape=[jax.ShapeDtypeStruct((BLOCKS, part, size), jnp.float32)]
        + [jax.ShapeDtypeStruct((BLOCKS, part, size), jnp.bfloat16)] * (RING - 1),
        in_specs=[smem] * 3
        + [pl.BlockSpec(memory_space=pltpu.HBM)] * len(units)
        + [vmem] * RING,
        out_specs=[vmem] * RING,
        scratch_shapes=[
            pltpu.VMEM((SUMS, part, size), jnp.bfloat16),
            pltpu.VMEM((SUMS + 1, part, size), jnp.float32),
            pltpu.VMEM((BLOCKS * slots, size, size), jnp.bfloat16),
            pltpu.SemaphoreType.DMA((len(units),)),
        ],
        compiler_params=pltpu.CompilerParams(vmem_limit_bytes=32 << 20),
        name="apply_tiles",
    )

    def apply_matrix(vectors, gathered=None):
        low = vectors.astype(jnp.bfloat16)
        gathered = gathered or gather_vectors(low)
        total, *partial = apply_tiles(
            jobs, marks, where, *stored, low, *(gathered[d] for d in (1, 2, 3))
        )
        sent = [exchange(partial[d - 1], d, 1) for d in (2, 1, 3)]
        for piece in sent:
            total = total + piece.astype(jnp.float32)
        return total + swap(total, "core")

    half_width = (bounds[2] - bounds[1]) * 0.5
    center = (bounds[2] + bounds[1]) * 0.5
    sigma_one = half_width / (bounds[0] - center)
    previous = start
    current = (apply_matrix(start, first_gathered) - center * start) * (sigma_one / half_width)
    sigma = sigma_one
    for _ in range(DEGREE - 1):
        sigma_next = 1.0 / (2.0 / sigma_one - sigma)
        product = apply_matrix(current)
        following = (product - center * current) * (2.0 * sigma_next / half_width) - (
            sigma * sigma_next
        ) * previous
        previous = current
        current = following
        sigma = sigma_next
    keep = jnp.where(core == 0, current[:CHIPS], current[CHIPS:])
    back = lax.all_to_all(keep, GROUP, 0, 0)
    return back.reshape(width, size).T


def solution(mesh):
    fine = Mesh(mesh.devices.reshape(tuple(SIZES.values())), tuple(SIZES))
    row, col = ("yl", "zh", "zl", "core"), ("x", "yh")
    placed = (
        P(row + col, None),
        P(row, col, None, None, None),
        P(row, col, None),
        P(row, col, None),
        P(),
    )
    return jax.shard_map(
        local, mesh=fine, in_specs=placed, out_specs=P(row + col, None), check_vma=False
    )
```

```python
import functools

import jax
import jax.numpy as jnp
from jax import lax
from jax.experimental import pallas as pl
from jax.experimental.pallas import tpu as pltpu
from jax.sharding import Mesh
from jax.sharding import PartitionSpec as P

DEGREE = 4
BATCH = 32
SIZES = {"yl": 2, "zh": 4, "zl": 2, "core": 2, "x": 4, "yh": 2}
GROUP = ("yl", "yh", "zl")
CHIPS = 8
BLOCKS = 2 * CHIPS
RING = 4
SUMS = RING * BLOCKS
LIST = 320


def around_y(array):
    pairs = []
    for low in range(2):
        for core in range(2):
            for high in range(2):
                target = (high * 2 + low - 1 + 2 * core) % 4
                pairs.append(
                    (
                        (low * 2 + core) * 2 + high,
                        (target % 2 * 2 + core) * 2 + target // 2,
                    )
                )
    return lax.ppermute(array, ("yl", "core", "yh"), pairs)


def swap(array, axis):
    return lax.ppermute(array, axis, [(0, 1), (1, 0)])


def exchange(array, step, x_core):
    pairs = []
    for high in range(RING):
        for core in range(2):
            for place in range(RING):
                if core == x_core:
                    target = (high * 2 + core) * RING + (place + step) % RING
                else:
                    target = ((high + step) % RING * 2 + core) * RING + place
                pairs.append(((high * 2 + core) * RING + place, target))
    return lax.ppermute(array, ("zh", "core", "x"), pairs)


def gather_vectors(low):
    return {d: exchange(low, -d, 0) for d in (2, 1, 3)}


def list_kernel(slots, codes, jobs, marks):
    def source(unit, found):
        def slot(t, found):
            code = codes[unit * slots + t]
            jobs[found] = code
            return found + jnp.where(code >= 0, 1, 0)

        found = lax.fori_loop(0, slots, slot, found)
        marks[unit] = found // BATCH
        return found

    found = lax.fori_loop(0, BLOCKS, source, jnp.int32(0))
    for extra in range(BATCH):
        jobs[found + extra] = SUMS
    marks[BLOCKS - 1] = (found + BATCH - 1) // BATCH


def apply_kernel(slots, units, jobs, marks, where, *refs):
    pieces, refs = refs[: len(units)], refs[len(units) :]
    taken, given = refs[:RING], refs[RING : 2 * RING]
    vectors, sums, tiles, arrived = refs[2 * RING :]
    copies, ends = [], []
    for k, (piece, count) in enumerate(zip(pieces, units)):
        part = pl.ds((ends[-1] if ends else 0) * slots, count * slots)
        copies.append(pltpu.make_async_copy(piece, tiles.at[part], arrived.at[k]))
        copies[-1].start()
        ends.append((ends[-1] if ends else 0) + count)
    for d in range(RING):
        vectors[d * BLOCKS : (d + 1) * BLOCKS] = taken[d][...]
    sums[...] = jnp.zeros_like(sums)

    def batches(first, last, contract):
        def batch(step, carry):
            products = []
            for k in range(BATCH):
                job = jobs[step * BATCH + k]
                products.append(
                    (
                        job & 255,
                        lax.dot_general(
                            vectors[(job >> 8) & 255],
                            tiles[job >> 16],
                            (((1,), (contract,)), ((), ())),
                            preferred_element_type=jnp.float32,
                        ),
                    )
                )
            for spot, product in products:
                sums[spot] += product
            return carry

        lax.fori_loop(first, last, batch, 0)

    first = 0
    for copy, end in zip(copies, ends):
        copy.wait()
        last = marks[end - 1]

        @pl.when(where[0] == 0)
        def _():
            batches(first, last, 0)

        @pl.when(where[0] != 0)
        def _():
            batches(first, last, 1)

        first = last

    for d in range(RING):
        given[d][...] = sums[d * BLOCKS : (d + 1) * BLOCKS].astype(given[d].dtype)


def local(start_block, tiles, tile_rows, tile_cols, bounds):
    size, width = start_block.shape
    slots = tiles.shape[2]
    part = width // CHIPS
    spot = {name: lax.axis_index(name) for name in SIZES}
    core = spot["core"]
    where = core.reshape(1).astype(jnp.int32)

    own_tiles = tiles.reshape(slots, size, size)
    places = jnp.concatenate(
        [tile_rows.reshape(1, slots), tile_cols.reshape(1, slots)]
    ).astype(jnp.float32)
    places = jnp.pad(places, ((0, 6), (0, size - slots)))
    message = jnp.concatenate(
        [
            start_block.T.reshape(CHIPS, part, size),
            jnp.broadcast_to(places[None], (CHIPS, 8, size)),
        ],
        axis=1,
    )
    def in_order(mine, theirs):
        return jnp.concatenate(
            [jnp.where(core == 0, mine, theirs), jnp.where(core == 0, theirs, mine)]
        )

    fellow = swap(own_tiles, "core")
    message, pair = lax.optimization_barrier((message, in_order(own_tiles, fellow)))
    around = around_y(pair)
    mine = lax.all_to_all(message, GROUP, 0, 0)
    theirs = swap(mine, "core")
    first = jnp.where(core == 0, mine, theirs)
    second = jnp.where(core == 0, theirs, mine)
    dealt = jnp.concatenate([first, second])
    start = dealt[:, :part]
    meta = dealt[:, part : part + 2, :slots].astype(jnp.int32)

    beside = swap(own_tiles, "zl")
    beside_fellow = swap(beside, "core")
    onward, dealt = lax.optimization_barrier(
        (jnp.where(core == 0, around[:slots], around[slots:]), dealt)
    )
    over = around_y(onward)
    low_start = dealt[:, :part].astype(jnp.bfloat16)
    first_gathered = gather_vectors(low_start)
    over, beside_pair, first_gathered = lax.optimization_barrier(
        (over, in_order(beside, beside_fellow), first_gathered)
    )
    beside_around = around_y(beside_pair)
    beside_over = swap(over, "zl")
    units = [1, 1, 1, 1, 2, 2, 1, 1, 2, 2, 1, 1]
    on_y, on_low = spot["yh"] * 2 + spot["yl"], spot["zl"]

    def unit(along, low, core_of):
        y = (on_y + along) % 4
        return core_of * CHIPS + (y % 2 * 2 + y // 2) * 2 + (on_low + low) % 2

    ahead = 1 - 2 * core
    held = [unit(0, low, c) for low in range(2) for c in (core, 1 - core)]
    for low in range(2):
        held += [unit(step, low, c) for step in (ahead, -ahead) for c in range(2)]
        held += [unit(2, low, c) for c in (core, 1 - core)]
    held = jnp.stack(held)

    group, member = meta >> 3, meta & 7
    block = (group & 1) * CHIPS + (
        ((group >> 4) * 2 + (member & 1)) * 2 + ((group >> 1) & 1)
    )
    near = ((member[:, 0] >> 1) - spot["x"] & 3) * BLOCKS + block[:, 0]
    far = ((group[:, 1] >> 2) - spot["zh"] & 3) * BLOCKS + block[:, 1]
    spots = jnp.where(core == 0, near << 8 | far, far << 8 | near)
    spots = jnp.where(meta[:, 0] >= 0, spots, -1)
    matches = held[:, None] == jnp.arange(BLOCKS, dtype=jnp.int32)[None]
    spots = jnp.sum(jnp.where(matches[:, :, None], spots[None], 0), axis=1)
    lies = jnp.arange(BLOCKS * slots, dtype=jnp.int32)
    codes = jnp.where(spots.reshape(-1) >= 0, lies << 16 | spots.reshape(-1), -1)

    smem = pl.BlockSpec(memory_space=pltpu.SMEM)
    vmem = pl.BlockSpec(memory_space=pltpu.VMEM)
    jobs, marks = pl.pallas_call(
        functools.partial(list_kernel, slots),
        out_shape=(
            jax.ShapeDtypeStruct((LIST,), jnp.int32),
            jax.ShapeDtypeStruct((BLOCKS,), jnp.int32),
        ),
        in_specs=[smem],
        out_specs=(smem, smem),
        name="list_jobs",
    )(codes)
    beside_around, beside_over, jobs, marks = lax.optimization_barrier(
        (beside_around, beside_over, jobs, marks)
    )
    pieces = [own_tiles, fellow, beside, beside_fellow, around, swap(around, "core")]
    pieces += [over, swap(over, "core"), beside_around, swap(beside_around, "core")]
    pieces += [beside_over, swap(beside_over, "core")]
    stored = [pltpu.with_memory_space_constraint(p, pltpu.HBM) for p in pieces]
    apply_tiles = pl.pallas_call(
        functools.partial(apply_kernel, slots, units),
        out_shape=[jax.ShapeDtypeStruct((BLOCKS, part, size), jnp.float32)]
        + [jax.ShapeDtypeStruct((BLOCKS, part, size), jnp.bfloat16)] * (RING - 1),
        in_specs=[smem] * 3
        + [pl.BlockSpec(memory_space=pltpu.HBM)] * len(units)
        + [vmem] * RING,
        out_specs=[vmem] * RING,
        scratch_shapes=[
            pltpu.VMEM((SUMS, part, size), jnp.bfloat16),
            pltpu.VMEM((SUMS + 1, part, size), jnp.float32),
            pltpu.VMEM((BLOCKS * slots, size, size), jnp.bfloat16),
            pltpu.SemaphoreType.DMA((len(units),)),
        ],
        compiler_params=pltpu.CompilerParams(vmem_limit_bytes=32 << 20),
        name="apply_tiles",
    )

    def apply_matrix(vectors, gathered=None):
        low = vectors.astype(jnp.bfloat16)
        gathered = gathered or gather_vectors(low)
        total, *partial = apply_tiles(
            jobs, marks, where, *stored, low, *(gathered[d] for d in (1, 2, 3))
        )
        sent = [exchange(partial[d - 1], d, 1) for d in (2, 1, 3)]
        for piece in sent:
            total = total + piece.astype(jnp.float32)
        return total + swap(total, "core")

    half_width = (bounds[2] - bounds[1]) * 0.5
    center = (bounds[2] + bounds[1]) * 0.5
    sigma_one = half_width / (bounds[0] - center)
    previous = start
    current = (apply_matrix(start, first_gathered) - center * start) * (sigma_one / half_width)
    sigma = sigma_one
    for _ in range(DEGREE - 1):
        sigma_next = 1.0 / (2.0 / sigma_one - sigma)
        product = apply_matrix(current)
        following = (product - center * current) * (2.0 * sigma_next / half_width) - (
            sigma * sigma_next
        ) * previous
        previous = current
        current = following
        sigma = sigma_next
    keep = jnp.where(core == 0, current[:CHIPS], current[CHIPS:])
    back = lax.all_to_all(keep, GROUP, 0, 0)
    return back.reshape(width, size).T


def solution(mesh):
    fine = Mesh(mesh.devices.reshape(tuple(SIZES.values())), tuple(SIZES))
    row, col = ("yl", "zh", "zl", "core"), ("x", "yh")
    placed = (
        P(row + col, None),
        P(row, col, None, None, None),
        P(row, col, None),
        P(row, col, None),
        P(),
    )
    return jax.shard_map(
        local, mesh=fine, in_specs=placed, out_specs=P(row + col, None), check_vma=False
    )
```

```python
import functools

import jax
import jax.numpy as jnp
from jax import lax
from jax.experimental import pallas as pl
from jax.experimental.pallas import tpu as pltpu
from jax.sharding import Mesh
from jax.sharding import PartitionSpec as P

DEGREE = 4
BATCH = 32
STOPS = (4, 8, 12, 16)
SIZES = {"yl": 2, "zh": 4, "zl": 2, "core": 2, "x": 4, "yh": 2}
GROUP = ("yl", "yh", "zl")
CHIPS = 8
BLOCKS = 2 * CHIPS
RING = 4
SUMS = RING * BLOCKS
LIST = 320


def around_y(array):
    pairs = []
    for low in range(2):
        for core in range(2):
            for high in range(2):
                target = (high * 2 + low - 1 + 2 * core) % 4
                pairs.append(
                    (
                        (low * 2 + core) * 2 + high,
                        (target % 2 * 2 + core) * 2 + target // 2,
                    )
                )
    return lax.ppermute(array, ("yl", "core", "yh"), pairs)


def swap(array, axis):
    return lax.ppermute(array, axis, [(0, 1), (1, 0)])


def exchange(array, step, x_core):
    pairs = []
    for high in range(RING):
        for core in range(2):
            for place in range(RING):
                if core == x_core:
                    target = (high * 2 + core) * RING + (place + step) % RING
                else:
                    target = ((high + step) % RING * 2 + core) * RING + place
                pairs.append(((high * 2 + core) * RING + place, target))
    return lax.ppermute(array, ("zh", "core", "x"), pairs)


def gather_vectors(low):
    return {d: exchange(low, -d, 0) for d in (2, 1, 3)}


def list_kernel(slots, codes, jobs, marks):
    def source(unit, found):
        def slot(t, found):
            code = codes[unit * slots + t]
            jobs[found] = code
            return found + jnp.where(code >= 0, 1, 0)

        found = lax.fori_loop(0, slots, slot, found)
        marks[unit] = found // BATCH
        return found

    found = lax.fori_loop(0, BLOCKS, source, jnp.int32(0))
    for extra in range(BATCH):
        jobs[found + extra] = SUMS
    marks[BLOCKS - 1] = (found + BATCH - 1) // BATCH


def apply_kernel(slots, units, jobs, marks, where, *refs):
    pieces, refs = refs[: len(units)], refs[len(units) :]
    taken, given = refs[:RING], refs[RING : 2 * RING]
    vectors, sums, tiles, arrived = refs[2 * RING :]
    copies, ends = [], []
    for k, (piece, count) in enumerate(zip(pieces, units)):
        part = pl.ds((ends[-1] if ends else 0) * slots, count * slots)
        copies.append(pltpu.make_async_copy(piece, tiles.at[part], arrived.at[k]))
        copies[-1].start()
        ends.append((ends[-1] if ends else 0) + count)
    for d in range(RING):
        vectors[d * BLOCKS : (d + 1) * BLOCKS] = taken[d][...]
    sums[...] = jnp.zeros_like(sums)

    def batches(first, last, contract):
        def batch(step, carry):
            products = []
            for k in range(BATCH):
                job = jobs[step * BATCH + k]
                products.append(
                    (
                        job & 255,
                        lax.dot_general(
                            vectors[(job >> 8) & 255],
                            tiles[job >> 16],
                            (((1,), (contract,)), ((), ())),
                            preferred_element_type=jnp.float32,
                        ),
                    )
                )
            for spot, product in products:
                sums[spot] += product
            return carry

        lax.fori_loop(first, last, batch, 0)

    first = 0
    for copy, end in zip(copies, ends):
        copy.wait()
        if end not in STOPS:
            continue
        last = marks[end - 1]

        @pl.when(where[0] == 0)
        def _():
            batches(first, last, 0)

        @pl.when(where[0] != 0)
        def _():
            batches(first, last, 1)

        first = last

    for d in range(RING):
        given[d][...] = sums[d * BLOCKS : (d + 1) * BLOCKS].astype(given[d].dtype)


def local(start_block, tiles, tile_rows, tile_cols, bounds):
    size, width = start_block.shape
    slots = tiles.shape[2]
    part = width // CHIPS
    spot = {name: lax.axis_index(name) for name in SIZES}
    core = spot["core"]
    where = core.reshape(1).astype(jnp.int32)

    own_tiles = tiles.reshape(slots, size, size)
    places = jnp.concatenate(
        [tile_rows.reshape(1, slots), tile_cols.reshape(1, slots)]
    ).astype(jnp.float32)
    places = jnp.pad(places, ((0, 6), (0, size - slots)))
    message = jnp.concatenate(
        [
            start_block.T.reshape(CHIPS, part, size),
            jnp.broadcast_to(places[None], (CHIPS, 8, size)),
        ],
        axis=1,
    )
    def in_order(mine, theirs):
        return jnp.concatenate(
            [jnp.where(core == 0, mine, theirs), jnp.where(core == 0, theirs, mine)]
        )

    fellow = swap(own_tiles, "core")
    message, pair = lax.optimization_barrier((message, in_order(own_tiles, fellow)))
    around = around_y(pair)
    mine = lax.all_to_all(message, GROUP, 0, 0)
    theirs = swap(mine, "core")
    first = jnp.where(core == 0, mine, theirs)
    second = jnp.where(core == 0, theirs, mine)
    dealt = jnp.concatenate([first, second])
    start = dealt[:, :part]
    meta = dealt[:, part : part + 2, :slots].astype(jnp.int32)

    beside = swap(own_tiles, "zl")
    beside_fellow = swap(beside, "core")
    onward, dealt = lax.optimization_barrier(
        (jnp.where(core == 0, around[:slots], around[slots:]), dealt)
    )
    over = around_y(onward)
    low_start = dealt[:, :part].astype(jnp.bfloat16)
    first_gathered = gather_vectors(low_start)
    over, beside_pair, first_gathered = lax.optimization_barrier(
        (over, in_order(beside, beside_fellow), first_gathered)
    )
    beside_around = around_y(beside_pair)
    beside_over = swap(over, "zl")
    units = [1, 1, 1, 1, 2, 2, 1, 1, 2, 2, 1, 1]
    on_y, on_low = spot["yh"] * 2 + spot["yl"], spot["zl"]

    def unit(along, low, core_of):
        y = (on_y + along) % 4
        return core_of * CHIPS + (y % 2 * 2 + y // 2) * 2 + (on_low + low) % 2

    ahead = 1 - 2 * core
    held = [unit(0, low, c) for low in range(2) for c in (core, 1 - core)]
    for low in range(2):
        held += [unit(step, low, c) for step in (ahead, -ahead) for c in range(2)]
        held += [unit(2, low, c) for c in (core, 1 - core)]
    held = jnp.stack(held)

    group, member = meta >> 3, meta & 7
    block = (group & 1) * CHIPS + (
        ((group >> 4) * 2 + (member & 1)) * 2 + ((group >> 1) & 1)
    )
    near = ((member[:, 0] >> 1) - spot["x"] & 3) * BLOCKS + block[:, 0]
    far = ((group[:, 1] >> 2) - spot["zh"] & 3) * BLOCKS + block[:, 1]
    spots = jnp.where(core == 0, near << 8 | far, far << 8 | near)
    spots = jnp.where(meta[:, 0] >= 0, spots, -1)
    matches = held[:, None] == jnp.arange(BLOCKS, dtype=jnp.int32)[None]
    spots = jnp.sum(jnp.where(matches[:, :, None], spots[None], 0), axis=1)
    lies = jnp.arange(BLOCKS * slots, dtype=jnp.int32)
    codes = jnp.where(spots.reshape(-1) >= 0, lies << 16 | spots.reshape(-1), -1)

    smem = pl.BlockSpec(memory_space=pltpu.SMEM)
    vmem = pl.BlockSpec(memory_space=pltpu.VMEM)
    jobs, marks = pl.pallas_call(
        functools.partial(list_kernel, slots),
        out_shape=(
            jax.ShapeDtypeStruct((LIST,), jnp.int32),
            jax.ShapeDtypeStruct((BLOCKS,), jnp.int32),
        ),
        in_specs=[smem],
        out_specs=(smem, smem),
        name="list_jobs",
    )(codes)
    beside_around, beside_over, jobs, marks = lax.optimization_barrier(
        (beside_around, beside_over, jobs, marks)
    )
    pieces = [own_tiles, fellow, beside, beside_fellow, around, swap(around, "core")]
    pieces += [over, swap(over, "core"), beside_around, swap(beside_around, "core")]
    pieces += [beside_over, swap(beside_over, "core")]
    stored = [pltpu.with_memory_space_constraint(p, pltpu.HBM) for p in pieces]
    apply_tiles = pl.pallas_call(
        functools.partial(apply_kernel, slots, units),
        out_shape=[jax.ShapeDtypeStruct((BLOCKS, part, size), jnp.float32)]
        + [jax.ShapeDtypeStruct((BLOCKS, part, size), jnp.bfloat16)] * (RING - 1),
        in_specs=[smem] * 3
        + [pl.BlockSpec(memory_space=pltpu.HBM)] * len(units)
        + [vmem] * RING,
        out_specs=[vmem] * RING,
        scratch_shapes=[
            pltpu.VMEM((SUMS, part, size), jnp.bfloat16),
            pltpu.VMEM((SUMS + 1, part, size), jnp.float32),
            pltpu.VMEM((BLOCKS * slots, size, size), jnp.bfloat16),
            pltpu.SemaphoreType.DMA((len(units),)),
        ],
        compiler_params=pltpu.CompilerParams(vmem_limit_bytes=32 << 20),
        name="apply_tiles",
    )

    def apply_matrix(vectors, gathered=None):
        low = vectors.astype(jnp.bfloat16)
        gathered = gathered or gather_vectors(low)
        total, *partial = apply_tiles(
            jobs, marks, where, *stored, low, *(gathered[d] for d in (1, 2, 3))
        )
        sent = [exchange(partial[d - 1], d, 1) for d in (2, 1, 3)]
        for piece in sent:
            total = total + piece.astype(jnp.float32)
        return total + swap(total, "core")

    half_width = (bounds[2] - bounds[1]) * 0.5
    center = (bounds[2] + bounds[1]) * 0.5
    sigma_one = half_width / (bounds[0] - center)
    previous = start
    current = (apply_matrix(start, first_gathered) - center * start) * (sigma_one / half_width)
    sigma = sigma_one
    for _ in range(DEGREE - 1):
        sigma_next = 1.0 / (2.0 / sigma_one - sigma)
        product = apply_matrix(current)
        following = (product - center * current) * (2.0 * sigma_next / half_width) - (
            sigma * sigma_next
        ) * previous
        previous = current
        current = following
        sigma = sigma_next
    keep = jnp.where(core == 0, current[:CHIPS], current[CHIPS:])
    back = lax.all_to_all(keep, GROUP, 0, 0)
    return back.reshape(width, size).T


def solution(mesh):
    fine = Mesh(mesh.devices.reshape(tuple(SIZES.values())), tuple(SIZES))
    row, col = ("yl", "zh", "zl", "core"), ("x", "yh")
    placed = (
        P(row + col, None),
        P(row, col, None, None, None),
        P(row, col, None),
        P(row, col, None),
        P(),
    )
    return jax.shard_map(
        local, mesh=fine, in_specs=placed, out_specs=P(row + col, None), check_vma=False
    )
```

```python
import functools

import jax
import jax.numpy as jnp
from jax import lax
from jax.experimental import pallas as pl
from jax.experimental.pallas import tpu as pltpu
from jax.sharding import Mesh
from jax.sharding import PartitionSpec as P

DEGREE = 4
BATCH = 32
STOPS = (4, 8, 12, 16)
SIZES = {"yl": 2, "zh": 4, "zl": 2, "core": 2, "x": 4, "yh": 2}
GROUP = ("yl", "yh", "zl")
CHIPS = 8
BLOCKS = 2 * CHIPS
RING = 4
SUMS = RING * BLOCKS
LIST = 320


def around_y(array):
    pairs = []
    for low in range(2):
        for core in range(2):
            for high in range(2):
                target = (high * 2 + low - 1 + 2 * core) % 4
                pairs.append(
                    (
                        (low * 2 + core) * 2 + high,
                        (target % 2 * 2 + core) * 2 + target // 2,
                    )
                )
    return lax.ppermute(array, ("yl", "core", "yh"), pairs)


def swap(array, axis):
    return lax.ppermute(array, axis, [(0, 1), (1, 0)])


def exchange(array, step, x_core):
    pairs = []
    for high in range(RING):
        for core in range(2):
            for place in range(RING):
                if core == x_core:
                    target = (high * 2 + core) * RING + (place + step) % RING
                else:
                    target = ((high + step) % RING * 2 + core) * RING + place
                pairs.append(((high * 2 + core) * RING + place, target))
    return lax.ppermute(array, ("zh", "core", "x"), pairs)


def gather_vectors(low):
    return {d: exchange(low, -d, 0) for d in (2, 1, 3)}


def list_kernel(slots, codes, jobs, marks):
    def source(unit, found):
        def slot(t, found):
            code = codes[unit * slots + t]
            jobs[found] = code
            return found + jnp.where(code >= 0, 1, 0)

        found = lax.fori_loop(0, slots, slot, found)
        marks[unit] = found // BATCH
        return found

    found = lax.fori_loop(0, BLOCKS, source, jnp.int32(0))
    for extra in range(BATCH):
        jobs[found + extra] = SUMS
    marks[BLOCKS - 1] = (found + BATCH - 1) // BATCH


def apply_kernel(slots, units, jobs, marks, where, *refs):
    pieces, refs = refs[: len(units)], refs[len(units) :]
    taken, given = refs[:RING], refs[RING : 2 * RING]
    vectors, sums, tiles, arrived = refs[2 * RING :]
    copies, ends = [], []
    for k, (piece, count) in enumerate(zip(pieces, units)):
        part = pl.ds((ends[-1] if ends else 0) * slots, count * slots)
        copies.append(pltpu.make_async_copy(piece, tiles.at[part], arrived.at[k]))
        copies[-1].start()
        ends.append((ends[-1] if ends else 0) + count)
    for d in range(RING):
        vectors[d * BLOCKS : (d + 1) * BLOCKS] = taken[d][...]
    sums[...] = jnp.zeros_like(sums)

    def batches(first, last, contract):
        def batch(step, carry):
            products = []
            for k in range(BATCH):
                job = jobs[step * BATCH + k]
                products.append(
                    (
                        job & 255,
                        lax.dot_general(
                            vectors[(job >> 8) & 255],
                            tiles[job >> 16],
                            (((1,), (contract,)), ((), ())),
                            preferred_element_type=jnp.float32,
                        ),
                    )
                )
            for spot, product in products:
                sums[spot] += product
            return carry

        lax.fori_loop(first, last, batch, 0)

    first = 0
    for copy, end in zip(copies, ends):
        copy.wait()
        if end not in STOPS:
            continue
        last = marks[end - 1]

        @pl.when(where[0] == 0)
        def _():
            batches(first, last, 0)

        @pl.when(where[0] != 0)
        def _():
            batches(first, last, 1)

        first = last

    for d in range(RING):
        given[d][...] = sums[d * BLOCKS : (d + 1) * BLOCKS].astype(given[d].dtype)


def local(start_block, tiles, tile_rows, tile_cols, bounds):
    size, width = start_block.shape
    slots = tiles.shape[2]
    part = width // CHIPS
    spot = {name: lax.axis_index(name) for name in SIZES}
    core = spot["core"]
    where = core.reshape(1).astype(jnp.int32)

    own_tiles = tiles.reshape(slots, size, size)
    places = jnp.concatenate(
        [tile_rows.reshape(1, slots), tile_cols.reshape(1, slots)]
    ).astype(jnp.float32)
    places = jnp.pad(places, ((0, 6), (0, size - slots)))
    message = jnp.concatenate(
        [
            start_block.T.reshape(CHIPS, part, size),
            jnp.broadcast_to(places[None], (CHIPS, 8, size)),
        ],
        axis=1,
    )
    def in_order(mine, theirs):
        return jnp.concatenate(
            [jnp.where(core == 0, mine, theirs), jnp.where(core == 0, theirs, mine)]
        )

    fellow = swap(own_tiles, "core")
    around = around_y(in_order(own_tiles, fellow))
    beside = swap(own_tiles, "zl")
    beside_fellow = swap(beside, "core")
    onward, message = lax.optimization_barrier(
        (jnp.where(core == 0, around[:slots], around[slots:]), message)
    )
    over = around_y(onward)
    over, mine = lax.optimization_barrier(
        (over, lax.all_to_all(message, GROUP, 0, 0))
    )
    theirs = swap(mine, "core")
    first = jnp.where(core == 0, mine, theirs)
    second = jnp.where(core == 0, theirs, mine)
    dealt = jnp.concatenate([first, second])
    start = dealt[:, :part]
    meta = dealt[:, part : part + 2, :slots].astype(jnp.int32)

    over, beside_pair = lax.optimization_barrier(
        (over, in_order(beside, beside_fellow))
    )
    first_gathered = gather_vectors(dealt[:, :part].astype(jnp.bfloat16))
    beside_around = around_y(beside_pair)
    beside_over = swap(over, "zl")
    units = [1, 1, 1, 1, 2, 2, 1, 1, 2, 2, 1, 1]
    on_y, on_low = spot["yh"] * 2 + spot["yl"], spot["zl"]

    def unit(along, low, core_of):
        y = (on_y + along) % 4
        return core_of * CHIPS + (y % 2 * 2 + y // 2) * 2 + (on_low + low) % 2

    ahead = 1 - 2 * core
    held = [unit(0, low, c) for low in range(2) for c in (core, 1 - core)]
    for low in range(2):
        held += [unit(step, low, c) for step in (ahead, -ahead) for c in range(2)]
        held += [unit(2, low, c) for c in (core, 1 - core)]
    held = jnp.stack(held)

    group, member = meta >> 3, meta & 7
    block = (group & 1) * CHIPS + (
        ((group >> 4) * 2 + (member & 1)) * 2 + ((group >> 1) & 1)
    )
    near = ((member[:, 0] >> 1) - spot["x"] & 3) * BLOCKS + block[:, 0]
    far = ((group[:, 1] >> 2) - spot["zh"] & 3) * BLOCKS + block[:, 1]
    spots = jnp.where(core == 0, near << 8 | far, far << 8 | near)
    spots = jnp.where(meta[:, 0] >= 0, spots, -1)
    matches = held[:, None] == jnp.arange(BLOCKS, dtype=jnp.int32)[None]
    spots = jnp.sum(jnp.where(matches[:, :, None], spots[None], 0), axis=1)
    lies = jnp.arange(BLOCKS * slots, dtype=jnp.int32)
    codes = jnp.where(spots.reshape(-1) >= 0, lies << 16 | spots.reshape(-1), -1)

    smem = pl.BlockSpec(memory_space=pltpu.SMEM)
    vmem = pl.BlockSpec(memory_space=pltpu.VMEM)
    jobs, marks = pl.pallas_call(
        functools.partial(list_kernel, slots),
        out_shape=(
            jax.ShapeDtypeStruct((LIST,), jnp.int32),
            jax.ShapeDtypeStruct((BLOCKS,), jnp.int32),
        ),
        in_specs=[smem],
        out_specs=(smem, smem),
        name="list_jobs",
    )(codes)
    beside_around, beside_over, jobs, marks, first_gathered = lax.optimization_barrier(
        (beside_around, beside_over, jobs, marks, first_gathered)
    )
    pieces = [own_tiles, fellow, beside, beside_fellow, around, swap(around, "core")]
    pieces += [over, swap(over, "core"), beside_around, swap(beside_around, "core")]
    pieces += [beside_over, swap(beside_over, "core")]
    stored = [pltpu.with_memory_space_constraint(p, pltpu.HBM) for p in pieces]
    apply_tiles = pl.pallas_call(
        functools.partial(apply_kernel, slots, units),
        out_shape=[jax.ShapeDtypeStruct((BLOCKS, part, size), jnp.float32)]
        + [jax.ShapeDtypeStruct((BLOCKS, part, size), jnp.bfloat16)] * (RING - 1),
        in_specs=[smem] * 3
        + [pl.BlockSpec(memory_space=pltpu.HBM)] * len(units)
        + [vmem] * RING,
        out_specs=[vmem] * RING,
        scratch_shapes=[
            pltpu.VMEM((SUMS, part, size), jnp.bfloat16),
            pltpu.VMEM((SUMS + 1, part, size), jnp.float32),
            pltpu.VMEM((BLOCKS * slots, size, size), jnp.bfloat16),
            pltpu.SemaphoreType.DMA((len(units),)),
        ],
        compiler_params=pltpu.CompilerParams(vmem_limit_bytes=32 << 20),
        name="apply_tiles",
    )

    def apply_matrix(vectors, gathered=None):
        low = vectors.astype(jnp.bfloat16)
        gathered = gathered or gather_vectors(low)
        total, *partial = apply_tiles(
            jobs, marks, where, *stored, low, *(gathered[d] for d in (1, 2, 3))
        )
        sent = [exchange(partial[d - 1], d, 1) for d in (2, 1, 3)]
        for piece in sent:
            total = total + piece.astype(jnp.float32)
        return total + swap(total, "core")

    half_width = (bounds[2] - bounds[1]) * 0.5
    center = (bounds[2] + bounds[1]) * 0.5
    sigma_one = half_width / (bounds[0] - center)
    previous = start
    current = (apply_matrix(start, first_gathered) - center * start) * (sigma_one / half_width)
    sigma = sigma_one
    for _ in range(DEGREE - 1):
        sigma_next = 1.0 / (2.0 / sigma_one - sigma)
        product = apply_matrix(current)
        following = (product - center * current) * (2.0 * sigma_next / half_width) - (
            sigma * sigma_next
        ) * previous
        previous = current
        current = following
        sigma = sigma_next
    keep = jnp.where(core == 0, current[:CHIPS], current[CHIPS:])
    back = lax.all_to_all(keep, GROUP, 0, 0)
    return back.reshape(width, size).T


def solution(mesh):
    fine = Mesh(mesh.devices.reshape(tuple(SIZES.values())), tuple(SIZES))
    row, col = ("yl", "zh", "zl", "core"), ("x", "yh")
    placed = (
        P(row + col, None),
        P(row, col, None, None, None),
        P(row, col, None),
        P(row, col, None),
        P(),
    )
    return jax.shard_map(
        local, mesh=fine, in_specs=placed, out_specs=P(row + col, None), check_vma=False
    )
```

```python
import functools

import jax
import jax.numpy as jnp
from jax import lax
from jax.experimental import pallas as pl
from jax.experimental.pallas import tpu as pltpu
from jax.sharding import Mesh
from jax.sharding import PartitionSpec as P

DEGREE = 4
BATCH = 32
STOPS = (4, 8, 12, 16)
SIZES = {"yl": 2, "zh": 4, "zl": 2, "core": 2, "x": 4, "yh": 2}
GROUP = ("yl", "yh", "zl")
CHIPS = 8
BLOCKS = 2 * CHIPS
RING = 4
SUMS = RING * BLOCKS
LIST = 320


def around_y(array):
    pairs = []
    for low in range(2):
        for core in range(2):
            for high in range(2):
                target = (high * 2 + low - 1 + 2 * core) % 4
                pairs.append(
                    (
                        (low * 2 + core) * 2 + high,
                        (target % 2 * 2 + core) * 2 + target // 2,
                    )
                )
    return lax.ppermute(array, ("yl", "core", "yh"), pairs)


def swap(array, axis):
    return lax.ppermute(array, axis, [(0, 1), (1, 0)])


def exchange(array, step, x_core):
    pairs = []
    for high in range(RING):
        for core in range(2):
            for place in range(RING):
                if core == x_core:
                    target = (high * 2 + core) * RING + (place + step) % RING
                else:
                    target = ((high + step) % RING * 2 + core) * RING + place
                pairs.append(((high * 2 + core) * RING + place, target))
    return lax.ppermute(array, ("zh", "core", "x"), pairs)


def gather_vectors(low):
    return {d: exchange(low, -d, 0) for d in (2, 1, 3)}


def list_kernel(slots, codes, jobs, marks):
    def source(unit, found):
        def slot(t, found):
            code = codes[unit * slots + t]
            jobs[found] = code
            return found + jnp.where(code >= 0, 1, 0)

        found = lax.fori_loop(0, slots, slot, found)
        marks[unit] = found // BATCH
        return found

    found = lax.fori_loop(0, BLOCKS, source, jnp.int32(0))
    for extra in range(BATCH):
        jobs[found + extra] = SUMS
    marks[BLOCKS - 1] = (found + BATCH - 1) // BATCH


def apply_kernel(slots, units, jobs, marks, where, *refs):
    pieces, refs = refs[: len(units)], refs[len(units) :]
    taken, given = refs[:RING], refs[RING : 2 * RING]
    vectors, sums, tiles, arrived = refs[2 * RING :]
    copies, ends = [], []
    for k, (piece, count) in enumerate(zip(pieces, units)):
        part = pl.ds((ends[-1] if ends else 0) * slots, count * slots)
        copies.append(pltpu.make_async_copy(piece, tiles.at[part], arrived.at[k]))
        copies[-1].start()
        ends.append((ends[-1] if ends else 0) + count)
    for d in range(RING):
        vectors[d * BLOCKS : (d + 1) * BLOCKS] = taken[d][...]
    sums[...] = jnp.zeros_like(sums)

    def batches(first, last, contract):
        def batch(step, carry):
            products = []
            for k in range(BATCH):
                job = jobs[step * BATCH + k]
                products.append(
                    (
                        job & 255,
                        lax.dot_general(
                            vectors[(job >> 8) & 255],
                            tiles[job >> 16],
                            (((1,), (contract,)), ((), ())),
                            preferred_element_type=jnp.float32,
                        ),
                    )
                )
            for spot, product in products:
                sums[spot] += product
            return carry

        lax.fori_loop(first, last, batch, 0)

    first = 0
    for copy, end in zip(copies, ends):
        copy.wait()
        if end not in STOPS:
            continue
        last = marks[end - 1]

        @pl.when(where[0] == 0)
        def _():
            batches(first, last, 0)

        @pl.when(where[0] != 0)
        def _():
            batches(first, last, 1)

        first = last

    for d in range(RING):
        given[d][...] = sums[d * BLOCKS : (d + 1) * BLOCKS].astype(given[d].dtype)


def local(start_block, tiles, tile_rows, tile_cols, bounds):
    size, width = start_block.shape
    slots = tiles.shape[2]
    part = width // CHIPS
    spot = {name: lax.axis_index(name) for name in SIZES}
    core = spot["core"]
    where = core.reshape(1).astype(jnp.int32)

    own_tiles = tiles.reshape(slots, size, size)
    places = jnp.concatenate(
        [tile_rows.reshape(1, slots), tile_cols.reshape(1, slots)]
    ).astype(jnp.float32)
    places = jnp.pad(places, ((0, 6), (0, size - slots)))
    message = jnp.concatenate(
        [
            start_block.T.reshape(CHIPS, part, size),
            jnp.broadcast_to(places[None], (CHIPS, 8, size)),
        ],
        axis=1,
    )
    def in_order(mine, theirs):
        return jnp.concatenate(
            [jnp.where(core == 0, mine, theirs), jnp.where(core == 0, theirs, mine)]
        )

    fellow = swap(own_tiles, "core")
    message, pair = lax.optimization_barrier((message, in_order(own_tiles, fellow)))
    around = around_y(pair)
    mine = lax.all_to_all(message, GROUP, 0, 0)
    theirs = swap(mine, "core")
    first = jnp.where(core == 0, mine, theirs)
    second = jnp.where(core == 0, theirs, mine)
    dealt = jnp.concatenate([first, second])
    start = dealt[:, :part]
    meta = dealt[:, part : part + 2, :slots].astype(jnp.int32)

    beside = swap(own_tiles, "zl")
    beside_fellow = swap(beside, "core")
    onward, dealt = lax.optimization_barrier(
        (jnp.where(core == 0, around[:slots], around[slots:]), dealt)
    )
    over = around_y(onward)
    low_start = dealt[:, :part].astype(jnp.bfloat16)
    first_gathered = gather_vectors(low_start)
    over, beside_pair, first_gathered = lax.optimization_barrier(
        (over, in_order(beside, beside_fellow), first_gathered)
    )
    beside_around = around_y(beside_pair)
    beside_over = swap(over, "zl")
    units = [1, 1, 1, 1, 2, 2, 1, 1, 2, 2, 1, 1]
    on_y, on_low = spot["yh"] * 2 + spot["yl"], spot["zl"]

    def unit(along, low, core_of):
        y = (on_y + along) % 4
        return core_of * CHIPS + (y % 2 * 2 + y // 2) * 2 + (on_low + low) % 2

    ahead = 1 - 2 * core
    held = [unit(0, low, c) for low in range(2) for c in (core, 1 - core)]
    for low in range(2):
        held += [unit(step, low, c) for step in (ahead, -ahead) for c in range(2)]
        held += [unit(2, low, c) for c in (core, 1 - core)]
    held = jnp.stack(held)

    group, member = meta >> 3, meta & 7
    block = (group & 1) * CHIPS + (
        ((group >> 4) * 2 + (member & 1)) * 2 + ((group >> 1) & 1)
    )
    near = ((member[:, 0] >> 1) - spot["x"] & 3) * BLOCKS + block[:, 0]
    far = ((group[:, 1] >> 2) - spot["zh"] & 3) * BLOCKS + block[:, 1]
    spots = jnp.where(core == 0, near << 8 | far, far << 8 | near)
    spots = jnp.where(meta[:, 0] >= 0, spots, -1)
    matches = held[:, None] == jnp.arange(BLOCKS, dtype=jnp.int32)[None]
    spots = jnp.sum(jnp.where(matches[:, :, None], spots[None], 0), axis=1)
    lies = jnp.arange(BLOCKS * slots, dtype=jnp.int32)
    codes = jnp.where(spots.reshape(-1) >= 0, lies << 16 | spots.reshape(-1), -1)

    smem = pl.BlockSpec(memory_space=pltpu.SMEM)
    vmem = pl.BlockSpec(memory_space=pltpu.VMEM)
    jobs, marks = pl.pallas_call(
        functools.partial(list_kernel, slots),
        out_shape=(
            jax.ShapeDtypeStruct((LIST,), jnp.int32),
            jax.ShapeDtypeStruct((BLOCKS,), jnp.int32),
        ),
        in_specs=[smem],
        out_specs=(smem, smem),
        name="list_jobs",
    )(codes)
    beside_around, beside_over, jobs, marks = lax.optimization_barrier(
        (beside_around, beside_over, jobs, marks)
    )
    pieces = [own_tiles, fellow, beside, beside_fellow, around, swap(around, "core")]
    pieces += [over, swap(over, "core"), beside_around, swap(beside_around, "core")]
    pieces += [beside_over, swap(beside_over, "core")]
    stored = [pltpu.with_memory_space_constraint(p, pltpu.HBM) for p in pieces]
    apply_tiles = pl.pallas_call(
        functools.partial(apply_kernel, slots, units),
        out_shape=[jax.ShapeDtypeStruct((BLOCKS, part, size), jnp.float32)]
        + [jax.ShapeDtypeStruct((BLOCKS, part, size), jnp.bfloat16)] * (RING - 1),
        in_specs=[smem] * 3
        + [pl.BlockSpec(memory_space=pltpu.HBM)] * len(units)
        + [vmem] * RING,
        out_specs=[vmem] * RING,
        scratch_shapes=[
            pltpu.VMEM((SUMS, part, size), jnp.bfloat16),
            pltpu.VMEM((SUMS + 1, part, size), jnp.float32),
            pltpu.VMEM((BLOCKS * slots, size, size), jnp.bfloat16),
            pltpu.SemaphoreType.DMA((len(units),)),
        ],
        compiler_params=pltpu.CompilerParams(vmem_limit_bytes=32 << 20),
        name="apply_tiles",
    )

    def kept(blocks):
        return jnp.where(core == 0, blocks[:CHIPS], blocks[CHIPS:])

    def apply_matrix(vectors, gathered=None, is_last=False):
        low = vectors.astype(jnp.bfloat16)
        gathered = gathered or gather_vectors(low)
        total, *partial = apply_tiles(
            jobs, marks, where, *stored, low, *(gathered[d] for d in (1, 2, 3))
        )
        sent = [exchange(partial[d - 1], d, 1) for d in (2, 1, 3)]
        for piece in sent:
            total = total + piece.astype(jnp.float32)
        if is_last:
            return kept(total) + swap(
                jnp.where(core == 0, total[CHIPS:], total[:CHIPS]), "core"
            )
        return total + swap(total, "core")

    half_width = (bounds[2] - bounds[1]) * 0.5
    center = (bounds[2] + bounds[1]) * 0.5
    sigma_one = half_width / (bounds[0] - center)
    previous = start
    current = (apply_matrix(start, first_gathered) - center * start) * (sigma_one / half_width)
    sigma = sigma_one
    for turn in range(DEGREE - 1):
        sigma_next = 1.0 / (2.0 / sigma_one - sigma)
        is_last = turn == DEGREE - 2
        product = apply_matrix(current, is_last=is_last)
        if is_last:
            previous, current = kept(previous), kept(current)
        following = (product - center * current) * (2.0 * sigma_next / half_width) - (
            sigma * sigma_next
        ) * previous
        previous = current
        current = following
        sigma = sigma_next
    back = lax.all_to_all(current, GROUP, 0, 0)
    return back.reshape(width, size).T


def solution(mesh):
    fine = Mesh(mesh.devices.reshape(tuple(SIZES.values())), tuple(SIZES))
    row, col = ("yl", "zh", "zl", "core"), ("x", "yh")
    placed = (
        P(row + col, None),
        P(row, col, None, None, None),
        P(row, col, None),
        P(row, col, None),
        P(),
    )
    return jax.shard_map(
        local, mesh=fine, in_specs=placed, out_specs=P(row + col, None), check_vma=False
    )
```
